256 devices in a mesh: section: 64 (over z, x, core), expert: 4 (over y).
Axes of the slice: x: 4, y: 4, z: 8, core: 2. Of those that a mesh axis runs over, the one named last changes fastest.
Arguments:
- tokens: bfloat16 [1024, 6144], P('section', 'expert'), may hold values from -6 to 6
- gains: float32 [6144], replicated, may hold values from 0.1 to 1.9
- w_gate: bfloat16 [4, 6144, 16384], P('expert', None, 'section'), may hold values from -0.078125 to 0.078125
- w_up: bfloat16 [4, 6144, 16384], P('expert', None, 'section'), may hold values from -0.078125 to 0.078125
- w_down: bfloat16 [4, 16384, 6144], P('expert', 'section'), may hold values from -0.046875 to 0.046875
- expert_ids: int32 [1024, 2], replicated, may hold values from 0 to 3, all different within a row; in each aligned block of 16 rows (0 to 15, 16 to 31, ...) at most 12 rows name the same one
- gate_ints: int32 [1024, 2], replicated, may hold values from 1 to 65535
Outputs:
- mixed: bfloat16 [1024, 6144], P('section', 'expert')
The draws below stay inside these ranges and needn't reach their ends.
Inputs may be any that keep to these rules, and one draw needn't show every extreme that they name: `expert_ids`: in each aligned block of 16 token rows (the rows of one index of section), no expert is named by more than 12 rows.
All inputs are finite; a program needn't handle non-finite values.
Results may differ from the reference program's by a relative error of at most 0.0042.
Values may be sent and summed in bfloat16 or wider, within the bound.
No kernel may reach another device: no remote copies, remote signals or barrier semaphores. Data moves between devices by JAX's collectives and lax.ppermute only.
A program may use at most 128 MiB of HBM per device.

```python
import math
import jax
import jax.numpy as jnp
import numpy as np
from jax import lax

D = 6144
TOP = 2
TOK_DEV = 16
CAP = 12
HID = 16384
EXPERTS = 4
TOKENS = 1024


def set_ends(array, own_key, smallest, top_value):
    dims = array.shape
    index_at = [jax.random.randint(jax.random.fold_in(own_key, axis), (), 0, dims[axis]) for axis in range(len(dims))]
    array = array.at[tuple(index_at)].set(smallest)
    longest = dims.index(max(dims))
    index_at[longest] = (index_at[longest] + 1) % dims[longest]
    return array.at[tuple(index_at)].set(top_value)


def steps_of(stream_key, extent, split, low, high):
    loudness = 1.0
    for dim, parts in split:
        heights = jax.random.uniform(jax.random.fold_in(jax.random.fold_in(stream_key, 6), dim), (parts,), jnp.float32, low / len(split), high / len(split))
        loudness = loudness * jnp.repeat(jnp.exp(heights), extent[dim] // parts).reshape((-1,) + (1,) * (len(extent) - 1 - dim))
    return loudness


def assign_block(own_key, own, number, rows, count, top, bound, lean):
    order = jax.random.permutation(own_key, count)
    heavy_load, usual = load_shares(count, rows * top, bound, lean, True), load_shares(count, rows * top, bound, lean, False)
    places = jnp.arange(count)

    def named(tallies, offset_by):
        used = int((tallies > 0).sum())
        fixed = max(1, used // 4)
        moved = fixed + (places - fixed + offset_by * (used - fixed)) % max(1, count - fixed)
        return jnp.zeros((count,), jnp.int32).at[order[jnp.where(places < fixed, places, moved)]].set(jnp.asarray(tallies, jnp.int32))

    tallies = jnp.where(number % 4 == 0, named(heavy_load, number // 4), named(usual, number - number // 4 - 1))
    mixed = jax.random.permutation(jax.random.fold_in(own, 3), count)
    giver, sink = mixed[0:count // 2 * 2:2], mixed[1:count // 2 * 2:2]
    slack = jnp.minimum(tallies[giver] - 1, bound - tallies[sink]) // 2
    slack = jnp.where((giver == order[0]) | (sink == order[0]) | (tallies[sink] == 0), 0, jnp.maximum(slack, 0))
    moved = jax.random.randint(jax.random.fold_in(own, 4), (count // 2,), 0, 1 << 20) % (slack + 1)
    tallies = tallies.at[giver].add(-moved).at[sink].add(moved)
    labels = jnp.searchsorted(jnp.cumsum(tallies), jnp.arange(rows * top), side="right").astype(jnp.int32)
    listing = labels.reshape(top, rows).T
    listing = listing[jax.random.permutation(jax.random.fold_in(own, 1), rows)]
    offset_by = jax.random.randint(jax.random.fold_in(own, 2), (rows, 1), 0, top)
    return jnp.take_along_axis(listing, (jnp.arange(top)[None, :] + offset_by) % top, axis=1)


def load_shares(count, total, most, slope, full):
    portions = [(1 << 20) // math.isqrt(standing ** slope) + 1 for standing in range(1, count + 1)]
    largest = most if full else min(most, max(-(-total // count), total * portions[0] // sum(portions)))
    least = 1 if total - largest >= count - 1 else 0
    holding, surplus = [largest] + [least] * (count - 1), total - largest - least * (count - 1)
    while surplus > 0:
        movable = [i for i in range(1, count) if holding[i] < largest] or [i for i in range(1, count) if holding[i] < most]
        pool, left = sum([portions[i] for i in movable]), surplus
        for i in movable:
            extra = min(most - holding[i], max(1, left * portions[i] // pool), surplus)
            holding[i] = holding[i] + extra
            surplus = surplus - extra
    return np.array(holding)


def noise(rng, shape, scale, most, shards=(), kind=jnp.bfloat16):
    drawn = scale * jax.random.normal(rng, shape, jnp.float32)
    if shards:
        drawn = drawn * steps_of(rng, shape, shards, -0.22, 0.18)
    return jnp.clip(drawn, -most, most).astype(kind)


def setup_inputs(seed: int = 0) -> dict:
    splits = jax.random.split(jax.random.key(seed), 8)
    tokens = noise(splits[0], (TOKENS, D), 1.0, 6.0, ((0, 64), (1, 4)))
    gains = jnp.clip(1.0 + 0.18 * jax.random.normal(splits[1], (D,), jnp.float32), 0.1, 1.9)
    w_gate = noise(splits[2], (EXPERTS, D, HID), D ** -0.5, 0.078125, ((0, 4), (2, 64)))
    w_up = noise(splits[3], (EXPERTS, D, HID), D ** -0.5, 0.078125, ((0, 4), (2, 64)))
    w_down = noise(splits[4], (EXPERTS, HID, D), HID ** -0.5, 0.046875, ((0, 4), (1, 64)))
    expert_ids_keys = jax.random.split(jax.random.fold_in(splits[5], 1), TOKENS // TOK_DEV)
    expert_ids_turns = jax.random.permutation(jax.random.fold_in(splits[5], 3), TOKENS // TOK_DEV)
    expert_ids = jax.vmap(lambda own, number: assign_block(jax.random.fold_in(splits[5], 2), own, number, TOK_DEV, EXPERTS, TOP, CAP, 2))(expert_ids_keys, expert_ids_turns).reshape((TOKENS, TOP))
    gate_ints = set_ends(jax.random.randint(splits[6], (TOKENS, TOP), 1, 65536), jax.random.fold_in(splits[6], 1), 1, 65535).astype(jnp.int32)
    return dict(tokens=tokens, gains=gains, w_gate=w_gate, w_up=w_up, w_down=w_down, expert_ids=expert_ids, gate_ints=gate_ints)


def reference(tokens, gains, w_gate, w_up, w_down, expert_ids, gate_ints):
    floated = tokens.astype(jnp.float32)
    mean_sq = lax.optimization_barrier(jnp.mean(floated * floated, axis=-1, keepdims=True))
    normed = (floated * lax.rsqrt(mean_sq + 1e-05) * gains).astype(jnp.bfloat16)
    scaled = gate_ints.astype(jnp.float32) / 65536.0

    def one_expert(running, expert_no):
        gate_val = jnp.dot(normed, w_gate[expert_no], preferred_element_type=jnp.float32)
        up_val = jnp.dot(normed, w_up[expert_no], preferred_element_type=jnp.float32)
        hidden_act = (jax.nn.silu(gate_val) * up_val).astype(jnp.bfloat16)
        result = jnp.dot(hidden_act, w_down[expert_no], preferred_element_type=jnp.float32)
        weight = lax.optimization_barrier(jnp.sum(jnp.where(expert_ids == expert_no, scaled, 0.0), axis=-1))
        return (running + result * weight[:, None], None)
    initial = jnp.zeros(floated.shape, jnp.float32)
    running, _ = lax.scan(one_expert, initial, jnp.arange(EXPERTS, dtype=jnp.int32))
    return (floated + running).astype(jnp.bfloat16)
```

```python
import functools

import jax
import jax.numpy as jnp
from jax import lax
from jax.experimental import pallas as pl
from jax.experimental.pallas import tpu as pltpu
from jax.sharding import Mesh, PartitionSpec as P

CAP = 12
BF = jnp.bfloat16
F32 = jnp.float32


def shift(a, axis, by):
    n = lax.axis_size(axis)
    return lax.ppermute(a, axis, [(i, (i + by) % n) for i in range(n)])


def ffn_kernel(n_pieces, x_ref, *refs):
    pieces = [refs[j * n_pieces : (j + 1) * n_pieces] for j in range(4)]
    refs = refs[4 * n_pieces :]
    gains = refs[0]
    wide = refs[1:5]
    down = refs[5:7]
    outs = refs[7:11]
    rows, wide_vmem, down_vmem, act, gate_acc, up_acc, sems = refs[11:]
    quarter = rows.shape[2]
    x = x_ref[0]
    copies = []
    for j in range(4):
        start = pl.multiple_of(lax.rem(x + j, 4) * quarter, quarter)
        for i in range(4):
            copies.append(
                pltpu.make_async_copy(wide[i].at[pl.ds(start, quarter), :], wide_vmem.at[j, i], sems.at[j * 4 + i])
            )
    for j in range(4):
        start = pl.multiple_of(lax.rem(x + j, 4) * quarter, quarter)
        for i in range(2):
            copies.append(
                pltpu.make_async_copy(down[i].at[:, pl.ds(start, quarter)], down_vmem.at[j, i], sems.at[16 + j * 2 + i])
            )
    for copy in copies:
        copy.start()
    at = 0
    for i in range(n_pieces):
        count = pieces[0][i].shape[0]
        total = jnp.zeros((count, 1), F32)
        for j in range(4):
            val = pieces[j][i][...].astype(F32)
            total = total + jnp.sum(val * val, axis=1, keepdims=True)
        scale = lax.rsqrt(total / (4.0 * quarter) + 1e-05)
        for j in range(4):
            val = pieces[j][i][...].astype(F32)
            rows[j, at : at + count, :] = (val * scale * gains[j : j + 1, :]).astype(BF)
        at += count
    hid = wide_vmem.shape[3]
    for j in range(4):
        lhs = rows[j]
        for i in range(4):
            copies[j * 4 + i].wait()
            acc = gate_acc if i < 2 else up_acc
            cols = slice((i % 2) * hid, (i % 2 + 1) * hid)
            val = jnp.dot(lhs, wide_vmem[j, i], preferred_element_type=F32)
            if j == 0:
                acc[:, cols] = val
            else:
                acc[:, cols] += val
    gate = gate_acc[...]
    act[...] = (gate / (1.0 + jnp.exp(-gate)) * up_acc[...]).astype(BF)
    for j in range(4):
        copies[16 + j * 2].wait()
        copies[17 + j * 2].wait()
        val = jnp.dot(act[:, :hid], down_vmem[j, 0], preferred_element_type=F32)
        val = val + jnp.dot(act[:, hid:], down_vmem[j, 1], preferred_element_type=F32)
        outs[j][...] = val.astype(BF)


def ffn(x, pieces, gains, wide, down):
    n_pieces = len(pieces[0])
    count = sum(p.shape[0] for p in pieces[0])
    quarter = pieces[0][0].shape[1]
    hid = wide[0].shape[1]
    vmem = pl.BlockSpec(memory_space=pltpu.VMEM)
    hbm = pl.BlockSpec(memory_space=pl.ANY)
    flops = 2 * count * 4 * quarter * 2 * hid * 3
    return pl.pallas_call(
        functools.partial(ffn_kernel, n_pieces),
        out_shape=[jax.ShapeDtypeStruct((count, quarter), BF)] * 4,
        in_specs=[pl.BlockSpec(memory_space=pltpu.SMEM)] + [vmem] * (4 * n_pieces + 1) + [hbm] * 6,
        out_specs=[vmem] * 4,
        scratch_shapes=[
            pltpu.VMEM((4, count, quarter), BF),
            pltpu.VMEM((4, 4, quarter, hid), BF),
            pltpu.VMEM((4, 2, hid, quarter), BF),
            pltpu.VMEM((count, 2 * hid), BF),
            pltpu.VMEM((count, 2 * hid), F32),
            pltpu.VMEM((count, 2 * hid), F32),
            pltpu.SemaphoreType.DMA((24,)),
        ],
        compiler_params=pltpu.CompilerParams(vmem_limit_bytes=44 * 1024 * 1024),
        cost_estimate=pl.CostEstimate(
            flops=flops, bytes_accessed=24 * quarter * hid * 2, transcendentals=count * 2 * hid
        ),
    )(x, *[p for per_j in pieces for p in per_j], gains, *wide, *down)


def gather_x(a):
    return [a, shift(a, "x", -1), shift(a, "x", 2), shift(a, "x", 1)]


def reduce_x(outs):
    got = [shift(outs[1], "x", 1), shift(outs[2], "x", 2), shift(outs[3], "x", -1)]
    return outs[0].astype(F32) + got[0].astype(F32) + got[1].astype(F32) + got[2].astype(F32)


def body(tokens, gains, w_gate, w_up, w_down, expert_ids, gate_ints):
    z = lax.axis_index("z")
    x = lax.axis_index("x")
    c = lax.axis_index("c")
    y = lax.axis_index("y")
    tok, quarter = tokens.shape
    gate_w, up_w, down_w = w_gate[0], w_up[0], w_down[0]
    wide = [gate_w, shift(gate_w, "c", 1), up_w, shift(up_w, "c", 1)]
    down = [down_w, shift(down_w, "c", 1)]
    blocks = []
    for k in range(4):
        pairs = [(a * 4 + b, b * 4 + (a + k) % 4) for a in range(4) for b in range(4)]
        blocks.append(lax.ppermute(tokens, ("x", "y"), pairs))
    ids = lax.dynamic_index_in_dim(
        lax.dynamic_index_in_dim(expert_ids.reshape(8, 4, 2, tok, 2), z, 0, False), c, 1, False
    )
    ints = lax.dynamic_index_in_dim(
        lax.dynamic_index_in_dim(gate_ints.reshape(8, 4, 2, tok, 2), z, 0, False), c, 1, False
    )
    chosen = ids == y
    selected = jnp.any(chosen, axis=-1)
    weight = jnp.sum(jnp.where(chosen, ints.astype(F32) / 65536.0, 0.0), axis=-1)
    t_of = jnp.arange(tok)
    place = jnp.sum((t_of[None, None, :] < t_of[None, :, None]) & selected[:, None, :], axis=-1)
    hot = (place[:, None, :] == jnp.arange(CAP)[None, :, None]) & selected[:, None, :]
    k_of = jnp.arange(4)
    from_block = (k_of[:, None] == (y - k_of[None, :]) % 4)[:, None, :, None]
    pick = (hot[:, :, None, :] & from_block).astype(BF).reshape(4 * CAP, 4 * tok)
    to_block = (k_of[:, None] == (y + k_of[None, :]) % 4)[:, None, :, None]
    put = jnp.where(hot[:, :, None, :] & to_block, weight[:, None, None, :], 0.0).reshape(4 * CAP, 4 * tok)

    picked = jnp.dot(pick, jnp.concatenate(blocks, axis=0), preferred_element_type=F32).astype(BF)
    gains_rel = jnp.roll(gains.reshape(4, quarter), -x, axis=0)
    x_arr = x.astype(jnp.int32).reshape(1)
    half = quarter // 2
    p1, m1 = shift(picked, "z", -1), shift(picked, "z", 1)
    p2, m2 = shift(picked, "z", -2), shift(picked, "z", 2)
    own = gather_x(picked)
    near = gather_x(jnp.concatenate([p1, m1, p2, m2], axis=0))
    p3, m3 = shift(p2, "z", -1), shift(m2, "z", 1)
    far4 = jnp.concatenate([shift(p2[:, :half], "z", -2), shift(m2[:, half:], "z", 2)], axis=1)
    far = gather_x(jnp.concatenate([p3, m3, far4], axis=0))

    out_near = ffn(x_arr, [[own[j], near[j]] for j in range(4)], gains_rel, wide, down)
    out_far = ffn(x_arr, [[far[j]] for j in range(4)], gains_rel, wide, down)

    n = picked.shape[0]
    sum_near = reduce_x(out_near)
    sum_far = reduce_x(out_far)
    far_bf = sum_far.astype(BF)
    got_p3 = shift(far_bf[:n], "z", 1)
    got_m3 = shift(far_bf[n : 2 * n], "z", -1)
    got_p4 = shift(far_bf[2 * n :, :half], "z", 2)
    got_m4 = shift(far_bf[2 * n :, half:], "z", -2)
    zero = jnp.zeros((n, half), F32)
    near_p2 = sum_near[3 * n : 4 * n] + got_p3.astype(F32) + jnp.concatenate([got_p4.astype(F32), zero], axis=1)
    near_m2 = sum_near[4 * n :] + got_m3.astype(F32) + jnp.concatenate([zero, got_m4.astype(F32)], axis=1)
    got = [
        shift(sum_near[n : 2 * n].astype(BF), "z", 1),
        shift(sum_near[2 * n : 3 * n].astype(BF), "z", -1),
        shift(near_p2.astype(BF), "z", 2),
        shift(near_m2.astype(BF), "z", -2),
    ]
    slots = sum_near[:n]
    for part in got:
        slots = slots + part.astype(F32)
    terms = lax.dot_general(
        put, slots, (((0,), (0,)), ((), ())), precision=lax.Precision.HIGHEST, preferred_element_type=F32
    ).astype(BF)
    total = tokens.astype(F32)
    for k in range(4):
        pairs = [(a * 4 + e, ((e + k) % 4) * 4 + a) for a in range(4) for e in range(4)]
        total = total + lax.ppermute(terms[k * tok : (k + 1) * tok], ("x", "y"), pairs).astype(F32)
    return total.astype(BF)


def solution(mesh):
    fine = Mesh(mesh.devices.reshape(8, 4, 2, 4), ("z", "x", "c", "y"))
    section = ("z", "x", "c")
    in_specs = (
        P(section, "y"),
        P(),
        P("y", None, section),
        P("y", None, section),
        P("y", section, None),
        P(),
        P(),
    )
    return jax.shard_map(body, mesh=fine, in_specs=in_specs, out_specs=P(section, "y"), check_vma=False)
```

```python
import functools

import jax
import jax.numpy as jnp
from jax import lax
from jax.experimental import pallas as pl
from jax.experimental.pallas import tpu as pltpu
from jax.sharding import Mesh, PartitionSpec as P

CAP = 12
BF = jnp.bfloat16
F32 = jnp.float32


def shift(a, axis, by):
    n = lax.axis_size(axis)
    return lax.ppermute(a, axis, [(i, (i + by) % n) for i in range(n)])


def ffn_kernel(counts, x_ref, *refs):
    refs = list(refs)
    pieces = [[refs.pop(0) for _ in per_j] for per_j in counts]
    gains, refs = refs[:4], refs[4:]
    wide, refs = refs[:4], refs[4:]
    down, refs = refs[:2], refs[2:]
    outs, refs = refs[:5], refs[5:]
    rows, act, gate_acc, up_acc = refs
    _, total_rows, quarter = rows.shape
    x = x_ref[0]
    for j in range(4):
        at = 0
        for piece, count in zip(pieces[j], counts[j]):
            rows[j, at : at + count, :] = piece[...]
            at += count
    step = 48
    for at in range(0, total_rows, step):
        total = jnp.zeros((step, 1), F32)
        for j in range(4):
            val = rows[j, at : at + step, :].astype(F32)
            total = total + jnp.sum(val * val, axis=1, keepdims=True)
        scale = lax.rsqrt(total / (4.0 * quarter) + 1e-05)
        for j in range(4):
            val = rows[j, at : at + step, :].astype(F32)
            rows[j, at : at + step, :] = (val * scale * gains[j][0:1, :]).astype(BF)
    hid = wide[0].shape[1]
    for j in range(4):
        start = pl.multiple_of(lax.rem(x + j, 4) * quarter, quarter)
        lhs = rows[j]
        for i in range(4):
            acc = gate_acc if i < 2 else up_acc
            cols = slice((i % 2) * hid, (i % 2 + 1) * hid)
            val = jnp.dot(lhs, wide[i][pl.ds(start, quarter), :], preferred_element_type=F32)
            if j == 0:
                acc[:, cols] = val
            else:
                acc[:, cols] += val
    gate = gate_acc[...]
    act[...] = (gate / (1.0 + jnp.exp(-gate)) * up_acc[...]).astype(BF)
    for j in range(4):
        start = pl.multiple_of(lax.rem(x + j, 4) * quarter, quarter)
        val = jnp.dot(act[:, :hid], down[0][:, pl.ds(start, quarter)], preferred_element_type=F32)
        val = val + jnp.dot(act[:, hid:], down[1][:, pl.ds(start, quarter)], preferred_element_type=F32)
        val = val.astype(BF)
        if j == 2:
            split = outs[2].shape[0]
            outs[2][...] = val[:split]
            outs[3][...] = val[split:]
        else:
            outs[j + j // 3][...] = val


def ffn(x, pieces, gains, wide, down):
    counts = tuple(tuple(p.shape[0] for p in per_j) for per_j in pieces)
    count = sum(counts[0])
    quarter = pieces[0][0].shape[1]
    hid = wide[0].shape[1]
    vmem = pl.BlockSpec(memory_space=pltpu.VMEM)
    n_pieces = sum(len(per_j) for per_j in counts)
    flops = 2 * count * 4 * quarter * 2 * hid * 3
    first = half_of(count)
    heights = [count, count, first, count - first, count]
    return pl.pallas_call(
        functools.partial(ffn_kernel, counts),
        out_shape=[jax.ShapeDtypeStruct((h, quarter), BF) for h in heights],
        in_specs=[pl.BlockSpec(memory_space=pltpu.SMEM)] + [vmem] * (n_pieces + 10),
        out_specs=[vmem] * 5,
        scratch_shapes=[
            pltpu.VMEM((4, count, quarter), BF),
            pltpu.VMEM((count, 2 * hid), BF),
            pltpu.VMEM((count, 2 * hid), F32),
            pltpu.VMEM((count, 2 * hid), F32),
        ],
        compiler_params=pltpu.CompilerParams(vmem_limit_bytes=13 * 1024 * 1024),
        cost_estimate=pl.CostEstimate(
            flops=flops, bytes_accessed=24 * quarter * hid * 2, transcendentals=count * 2 * hid
        ),
    )(x, *[p for per_j in pieces for p in per_j], *gains, *wide, *down)


def half_of(count):
    return (count // 32) * 16


def gather_x_first(a):
    return shift(a, "x", 1), shift(a, "x", -1)


def gather_x_last(a, left, right):
    h = half_of(a.shape[0])
    return [[a], [right], [shift(left[:h], "x", 1), shift(right[h:], "x", -1)], [left]]


def concat_rows(parts):
    def kernel(*refs):
        at = 0
        for ref in refs[:-1]:
            refs[-1][at : at + ref.shape[0], :] = ref[...]
            at += ref.shape[0]

    vmem = pl.BlockSpec(memory_space=pltpu.VMEM)
    shape = jax.ShapeDtypeStruct((sum(p.shape[0] for p in parts), parts[0].shape[1]), parts[0].dtype)
    params = pltpu.CompilerParams(vmem_limit_bytes=4 * 1024 * 1024)
    return pl.pallas_call(
        kernel, out_shape=shape, in_specs=[vmem] * len(parts), out_specs=vmem, compiler_params=params
    )(*parts)


def add_rows(base, part, at):
    def kernel(base_ref, part_ref, out_ref):
        del base_ref
        rows = slice(at, at + part.shape[0])
        out_ref[rows, :] = (out_ref[rows, :].astype(F32) + part_ref[...].astype(F32)).astype(BF)

    vmem = pl.BlockSpec(memory_space=pltpu.VMEM)
    return pl.pallas_call(
        kernel,
        out_shape=jax.ShapeDtypeStruct(base.shape, base.dtype),
        in_specs=[vmem, vmem],
        out_specs=vmem,
        input_output_aliases={0: 0},
        compiler_params=pltpu.CompilerParams(vmem_limit_bytes=4 * 1024 * 1024),
    )(base, part)


def reduce_x_first(outs):
    _, to_right, far_first, far_second, to_left = outs
    h = far_first.shape[0]
    return add_rows(to_right, shift(far_first, "x", 1), 0), add_rows(to_left, shift(far_second, "x", -1), h)


def reduce_x_last(mine, right_sum, left_sum):
    from_left = shift(right_sum, "x", 1)
    from_right = shift(left_sum, "x", -1)
    return mine.astype(F32) + from_left.astype(F32) + from_right.astype(F32)


def body(tokens, gains, w_gate, w_up, w_down, expert_ids, gate_ints):
    z = lax.axis_index("z")
    x = lax.axis_index("x")
    c = lax.axis_index("c")
    y = lax.axis_index("y")
    tok, quarter = tokens.shape
    gate_w, up_w, down_w = w_gate[0], w_up[0], w_down[0]
    blocks = []
    for k in range(4):
        pairs = [(a * 4 + b, b * 4 + (a + k) % 4) for a in range(4) for b in range(4)]
        blocks.append(lax.ppermute(tokens, ("x", "y"), pairs))
    def routed_rows(a):
        starts = [((z * 4 + (y - k) % 4) * 2 + c) * tok for k in range(4)]
        return jnp.concatenate([lax.dynamic_slice_in_dim(a, start, tok, 0) for start in starts], axis=0)

    chosen = routed_rows(expert_ids) == y
    selected = jnp.any(chosen, axis=-1)
    weight = jnp.sum(jnp.where(chosen, routed_rows(gate_ints).astype(F32) / 65536.0, 0.0), axis=-1)
    col = jnp.arange(4 * tok)
    earlier = (col[None, :] // tok == col[:, None] // tok) & (col[None, :] < col[:, None])
    place = jnp.sum(earlier & selected[None, :], axis=1)
    slot = (y - col // tok) % 4 * CAP + place
    hot = (slot[None, :] == jnp.arange(4 * CAP)[:, None]) & selected[None, :]
    pick = hot.astype(BF)
    put = jnp.where(hot, weight[None, :], 0.0)

    picked = jnp.dot(pick, jnp.concatenate(blocks, axis=0), preferred_element_type=F32).astype(BF)
    gains_rel = [
        lax.broadcast_in_dim(lax.dynamic_slice_in_dim(gains, (x + j) % 4 * quarter, quarter, 0), (8, quarter), (1,))
        for j in range(4)
    ]
    x_arr = x.astype(jnp.int32).reshape(1)
    picked, put, x_arr, gains_rel, gate_s, up_in = lax.optimization_barrier(
        (picked, put, x_arr, gains_rel, shift(gate_w, "c", 1), up_w)
    )
    up_s = shift(up_in, "c", 1)
    p1, m1 = shift(picked, "z", -1), shift(picked, "z", 1)
    p2, m2 = shift(picked, "z", -2), shift(picked, "z", 2)
    p1, m1, p2, m2, up_s, down_in = lax.optimization_barrier((p1, m1, p2, m2, up_s, down_w))
    wide = [gate_w, gate_s, up_w, up_s]
    down = [down_w, shift(down_in, "c", 1)]
    near = concat_rows([picked, p1, m1, p2, m2])
    near_left, near_right = gather_x_first(near)
    far_in, down_s = lax.optimization_barrier((picked, down[1]))
    down = [down_w, down_s]
    far = concat_rows([shift(far_in, "z", -3), shift(far_in, "z", 3), shift(far_in, "z", 4)])
    far_left, far_right = gather_x_first(far)
    x_near, far_left, far_right = lax.optimization_barrier((x_arr, far_left, far_right))
    far = gather_x_last(far, far_left, far_right)

    out_near = ffn(x_near, gather_x_last(near, near_left, near_right), gains_rel, wide, down)
    x_far, *out_near = lax.optimization_barrier((x_arr, *out_near))
    out_far = ffn(x_far, far, gains_rel, wide, down)

    n = picked.shape[0]
    sums_near = reduce_x_first(out_near)
    sums_near, out_far = lax.optimization_barrier((sums_near, out_far))
    sum_far = reduce_x_last(out_far[0], *reduce_x_first(out_far)).astype(BF)
    sum_near = reduce_x_last(out_near[0], *sums_near)
    slots = sum_near[:n]
    for i, by in enumerate((3, -3, 4)):
        slots = slots + shift(sum_far[i * n : (i + 1) * n], "z", by).astype(F32)
    for i, by in enumerate((1, -1, 2, -2)):
        slots = slots + shift(sum_near[(i + 1) * n : (i + 2) * n].astype(BF), "z", by).astype(F32)
    terms = lax.dot_general(
        put, slots, (((0,), (0,)), ((), ())), precision=lax.Precision.HIGHEST, preferred_element_type=F32
    ).astype(BF)
    total = tokens.astype(F32)
    for k in range(4):
        pairs = [(a * 4 + e, ((e - k) % 4) * 4 + a) for a in range(4) for e in range(4)]
        total = total + lax.ppermute(terms[k * tok : (k + 1) * tok], ("x", "y"), pairs).astype(F32)
    return total.astype(BF)


def solution(mesh):
    fine = Mesh(mesh.devices.reshape(8, 4, 2, 4), ("z", "x", "c", "y"))
    section = ("z", "x", "c")
    in_specs = (
        P(section, "y"),
        P(),
        P("y", None, section),
        P("y", None, section),
        P("y", section, None),
        P(),
        P(),
    )
    return jax.shard_map(body, mesh=fine, in_specs=in_specs, out_specs=P(section, "y"), check_vma=False)
```

```python
import functools

import jax
import jax.numpy as jnp
from jax import lax
from jax.experimental import pallas as pl
from jax.experimental.pallas import tpu as pltpu
from jax.sharding import Mesh, PartitionSpec as P

CAP = 12
BF = jnp.bfloat16
F32 = jnp.float32


def shift(a, axis, by):
    n = lax.axis_size(axis)
    return lax.ppermute(a, axis, [(i, (i + by) % n) for i in range(n)])


def ffn_kernel(counts, x_ref, *refs):
    refs = list(refs)
    pieces = [[refs.pop(0) for _ in per_j] for per_j in counts]
    gains, refs = refs[:4], refs[4:]
    wide, refs = refs[:4], refs[4:]
    down, refs = refs[:2], refs[2:]
    outs, refs = refs[:5], refs[5:]
    rows, act, gate_acc, up_acc = refs
    _, total_rows, quarter = rows.shape
    x = x_ref[0]
    for j in range(4):
        at = 0
        for piece, count in zip(pieces[j], counts[j]):
            rows[j, at : at + count, :] = piece[...]
            at += count
    step = 48
    for at in range(0, total_rows, step):
        total = jnp.zeros((step, 1), F32)
        for j in range(4):
            val = rows[j, at : at + step, :].astype(F32)
            total = total + jnp.sum(val * val, axis=1, keepdims=True)
        scale = lax.rsqrt(total / (4.0 * quarter) + 1e-05)
        for j in range(4):
            val = rows[j, at : at + step, :].astype(F32)
            rows[j, at : at + step, :] = (val * scale * gains[j][0:1, :]).astype(BF)
    hid = wide[0].shape[1]
    for j in range(4):
        start = pl.multiple_of(lax.rem(x + j, 4) * quarter, quarter)
        lhs = rows[j]
        for i in range(4):
            acc = gate_acc if i < 2 else up_acc
            cols = slice((i % 2) * hid, (i % 2 + 1) * hid)
            val = jnp.dot(lhs, wide[i][pl.ds(start, quarter), :], preferred_element_type=F32)
            if j == 0:
                acc[:, cols] = val
            else:
                acc[:, cols] += val
    gate = gate_acc[...]
    act[...] = (gate / (1.0 + jnp.exp(-gate)) * up_acc[...]).astype(BF)
    for j in range(4):
        start = pl.multiple_of(lax.rem(x + j, 4) * quarter, quarter)
        val = jnp.dot(act[:, :hid], down[0][:, pl.ds(start, quarter)], preferred_element_type=F32)
        val = val + jnp.dot(act[:, hid:], down[1][:, pl.ds(start, quarter)], preferred_element_type=F32)
        val = val.astype(BF)
        if j == 2:
            split = outs[2].shape[0]
            outs[2][...] = val[:split]
            outs[3][...] = val[split:]
        else:
            outs[j + j // 3][...] = val


def ffn(x, pieces, gains, wide, down):
    counts = tuple(tuple(p.shape[0] for p in per_j) for per_j in pieces)
    count = sum(counts[0])
    quarter = pieces[0][0].shape[1]
    hid = wide[0].shape[1]
    vmem = pl.BlockSpec(memory_space=pltpu.VMEM)
    n_pieces = sum(len(per_j) for per_j in counts)
    flops = 2 * count * 4 * quarter * 2 * hid * 3
    first = half_of(count)
    heights = [count, count, first, count - first, count]
    return pl.pallas_call(
        functools.partial(ffn_kernel, counts),
        out_shape=[jax.ShapeDtypeStruct((h, quarter), BF) for h in heights],
        in_specs=[pl.BlockSpec(memory_space=pltpu.SMEM)] + [vmem] * (n_pieces + 10),
        out_specs=[vmem] * 5,
        scratch_shapes=[
            pltpu.VMEM((4, count, quarter), BF),
            pltpu.VMEM((count, 2 * hid), BF),
            pltpu.VMEM((count, 2 * hid), F32),
            pltpu.VMEM((count, 2 * hid), F32),
        ],
        compiler_params=pltpu.CompilerParams(vmem_limit_bytes=13 * 1024 * 1024),
        cost_estimate=pl.CostEstimate(
            flops=flops, bytes_accessed=24 * quarter * hid * 2, transcendentals=count * 2 * hid
        ),
    )(x, *[p for per_j in pieces for p in per_j], *gains, *wide, *down)


def half_of(count):
    return (count // 32) * 16


def gather_x_first(a):
    return shift(a, "x", 1), shift(a, "x", -1)


def gather_x_last(a, left, right):
    h = half_of(a.shape[0])
    return [[a], [right], [shift(left[:h], "x", 1), shift(right[h:], "x", -1)], [left]]


def concat_rows(parts):
    def kernel(*refs):
        at = 0
        for ref in refs[:-1]:
            refs[-1][at : at + ref.shape[0], :] = ref[...]
            at += ref.shape[0]

    vmem = pl.BlockSpec(memory_space=pltpu.VMEM)
    shape = jax.ShapeDtypeStruct((sum(p.shape[0] for p in parts), parts[0].shape[1]), parts[0].dtype)
    params = pltpu.CompilerParams(vmem_limit_bytes=4 * 1024 * 1024)
    return pl.pallas_call(
        kernel, out_shape=shape, in_specs=[vmem] * len(parts), out_specs=vmem, compiler_params=params
    )(*parts)


def load_weights(weights):
    def kernel(*refs):
        n = len(refs) // 2
        copies = [pltpu.make_async_copy(refs[i], refs[n + i], refs[-1].at[i]) for i in range(n)]
        for copy in copies:
            copy.start()
        for copy in copies:
            copy.wait()

    n = len(weights)
    total = sum(w.size for w in weights) * 2
    return pl.pallas_call(
        kernel,
        out_shape=[jax.ShapeDtypeStruct(w.shape, w.dtype) for w in weights],
        in_specs=[pl.BlockSpec(memory_space=pl.ANY)] * n,
        out_specs=[pl.BlockSpec(memory_space=pltpu.VMEM)] * n,
        scratch_shapes=[pltpu.SemaphoreType.DMA((n,))],
        compiler_params=pltpu.CompilerParams(vmem_limit_bytes=4 * 1024 * 1024),
        cost_estimate=pl.CostEstimate(flops=0, bytes_accessed=2 * total, transcendentals=0),
    )(*weights)


def concat_far(p3, m3, p4, m4):
    def kernel(p3_ref, m3_ref, p4_ref, m4_ref, out_ref):
        n, half = p4_ref.shape
        out_ref[:n, :] = p3_ref[...]
        out_ref[n : 2 * n, :] = m3_ref[...]
        out_ref[2 * n :, :half] = p4_ref[...]
        out_ref[2 * n :, half:] = m4_ref[...]

    vmem = pl.BlockSpec(memory_space=pltpu.VMEM)
    shape = jax.ShapeDtypeStruct((3 * p3.shape[0], p3.shape[1]), p3.dtype)
    params = pltpu.CompilerParams(vmem_limit_bytes=4 * 1024 * 1024)
    return pl.pallas_call(
        kernel, out_shape=shape, in_specs=[vmem] * 4, out_specs=vmem, compiler_params=params
    )(p3, m3, p4, m4)


def add_rows(base, part, at):
    def kernel(base_ref, part_ref, out_ref):
        del base_ref
        rows = slice(at, at + part.shape[0])
        out_ref[rows, :] = (out_ref[rows, :].astype(F32) + part_ref[...].astype(F32)).astype(BF)

    vmem = pl.BlockSpec(memory_space=pltpu.VMEM)
    return pl.pallas_call(
        kernel,
        out_shape=jax.ShapeDtypeStruct(base.shape, base.dtype),
        in_specs=[vmem, vmem],
        out_specs=vmem,
        input_output_aliases={0: 0},
        compiler_params=pltpu.CompilerParams(vmem_limit_bytes=4 * 1024 * 1024),
    )(base, part)


def reduce_x_first(outs):
    _, to_right, far_first, far_second, to_left = outs
    h = far_first.shape[0]
    return add_rows(to_right, shift(far_first, "x", 1), 0), add_rows(to_left, shift(far_second, "x", -1), h)


def reduce_x_last(mine, right_sum, left_sum):
    from_left = shift(right_sum, "x", 1)
    from_right = shift(left_sum, "x", -1)
    return mine.astype(F32) + from_left.astype(F32) + from_right.astype(F32)


def body(tokens, gains, w_gate, w_up, w_down, expert_ids, gate_ints):
    z = lax.axis_index("z")
    x = lax.axis_index("x")
    c = lax.axis_index("c")
    y = lax.axis_index("y")
    tok, quarter = tokens.shape
    gate_w, up_w, down_w = w_gate[0], w_up[0], w_down[0]
    blocks = []
    for k in range(4):
        pairs = [(a * 4 + b, b * 4 + (a + k) % 4) for a in range(4) for b in range(4)]
        blocks.append(lax.ppermute(tokens, ("x", "y"), pairs))
    def routed_rows(a):
        starts = [((z * 4 + (y - k) % 4) * 2 + c) * tok for k in range(4)]
        return jnp.concatenate([lax.dynamic_slice_in_dim(a, start, tok, 0) for start in starts], axis=0)

    chosen = routed_rows(expert_ids) == y
    selected = jnp.any(chosen, axis=-1)
    weight = jnp.sum(jnp.where(chosen, routed_rows(gate_ints).astype(F32) / 65536.0, 0.0), axis=-1)
    col = jnp.arange(4 * tok)
    earlier = (col[None, :] // tok == col[:, None] // tok) & (col[None, :] < col[:, None])
    place = jnp.sum(earlier & selected[None, :], axis=1)
    slot = (y - col // tok) % 4 * CAP + place
    hot = (slot[None, :] == jnp.arange(4 * CAP)[:, None]) & selected[None, :]
    pick = hot.astype(BF)
    put = jnp.where(hot, weight[None, :], 0.0)

    picked = jnp.dot(pick, jnp.concatenate(blocks, axis=0), preferred_element_type=F32).astype(BF)
    gains_rel = [
        lax.broadcast_in_dim(lax.dynamic_slice_in_dim(gains, (x + j) % 4 * quarter, quarter, 0), (8, quarter), (1,))
        for j in range(4)
    ]
    x_arr = x.astype(jnp.int32).reshape(1)
    picked, put, x_arr, gains_rel, gate_s, up_in = lax.optimization_barrier(
        (picked, put, x_arr, gains_rel, shift(gate_w, "c", 1), up_w)
    )
    up_s = shift(up_in, "c", 1)
    p1, m1 = shift(picked, "z", -1), shift(picked, "z", 1)
    p2, m2 = shift(picked, "z", -2), shift(picked, "z", 2)
    p1, m1, p2, m2, up_s, down_in = lax.optimization_barrier((p1, m1, p2, m2, up_s, down_w))
    gate_v, up_v, down_v = load_weights([gate_w, up_w, down_w])
    wide = [gate_v, gate_s, up_v, up_s]
    down = [down_w, shift(down_in, "c", 1)]
    near = concat_rows([picked, p1, m1, p2, m2])
    near_left, near_right = gather_x_first(near)
    p2, m2, down_s = lax.optimization_barrier((p2, m2, down[1]))
    down = [down_v, down_s]
    half = quarter // 2
    p3, m3 = shift(p2, "z", -1), shift(m2, "z", 1)
    p4, m4 = shift(p2[:, :half], "z", -2), shift(m2[:, half:], "z", 2)
    far = concat_far(p3, m3, p4, m4)
    far_left, far_right = gather_x_first(far)
    x_near, far_left, far_right = lax.optimization_barrier((x_arr, far_left, far_right))
    far = gather_x_last(far, far_left, far_right)

    out_near = ffn(x_near, gather_x_last(near, near_left, near_right), gains_rel, wide, down)
    x_far, *out_near = lax.optimization_barrier((x_arr, *out_near))
    out_far = ffn(x_far, far, gains_rel, wide, down)

    n = picked.shape[0]
    sums_near = reduce_x_first(out_near)
    sums_near, out_far = lax.optimization_barrier((sums_near, out_far))
    sum_far = reduce_x_last(out_far[0], *reduce_x_first(out_far)).astype(BF)
    sum_near = reduce_x_last(out_near[0], *sums_near)
    slots = sum_near[:n]
    for i, by in enumerate((3, -3, 4)):
        slots = slots + shift(sum_far[i * n : (i + 1) * n], "z", by).astype(F32)
    for i, by in enumerate((1, -1, 2, -2)):
        slots = slots + shift(sum_near[(i + 1) * n : (i + 2) * n].astype(BF), "z", by).astype(F32)
    terms = lax.dot_general(
        put, slots, (((0,), (0,)), ((), ())), precision=lax.Precision.HIGHEST, preferred_element_type=F32
    ).astype(BF)
    total = tokens.astype(F32)
    for k in range(4):
        pairs = [(a * 4 + e, ((e - k) % 4) * 4 + a) for a in range(4) for e in range(4)]
        total = total + lax.ppermute(terms[k * tok : (k + 1) * tok], ("x", "y"), pairs).astype(F32)
    return total.astype(BF)


def solution(mesh):
    fine = Mesh(mesh.devices.reshape(8, 4, 2, 4), ("z", "x", "c", "y"))
    section = ("z", "x", "c")
    in_specs = (
        P(section, "y"),
        P(),
        P("y", None, section),
        P("y", None, section),
        P("y", section, None),
        P(),
        P(),
    )
    return jax.shard_map(body, mesh=fine, in_specs=in_specs, out_specs=P(section, "y"), check_vma=False)
```

```python
import functools

import jax
import jax.numpy as jnp
from jax import lax
from jax.experimental import pallas as pl
from jax.experimental.pallas import tpu as pltpu
from jax.sharding import Mesh, PartitionSpec as P

CAP = 12
BF = jnp.bfloat16
F32 = jnp.float32


def shift(a, axis, by):
    n = lax.axis_size(axis)
    return lax.ppermute(a, axis, [(i, (i + by) % n) for i in range(n)])


def ffn_kernel(counts, x_ref, *refs):
    refs = list(refs)
    pieces = [[refs.pop(0) for _ in per_j] for per_j in counts]
    gains, refs = refs[:4], refs[4:]
    wide, refs = refs[:4], refs[4:]
    down, refs = refs[:2], refs[2:]
    outs, refs = refs[:5], refs[5:]
    rows, act, gate_acc, up_acc = refs
    _, total_rows, quarter = rows.shape
    x = x_ref[0]
    for j in range(4):
        at = 0
        for piece, count in zip(pieces[j], counts[j]):
            rows[j, at : at + count, :] = piece[...]
            at += count
    step = 48
    for at in range(0, total_rows, step):
        total = jnp.zeros((step, 1), F32)
        for j in range(4):
            val = rows[j, at : at + step, :].astype(F32)
            total = total + jnp.sum(val * val, axis=1, keepdims=True)
        scale = lax.rsqrt(total / (4.0 * quarter) + 1e-05)
        for j in range(4):
            val = rows[j, at : at + step, :].astype(F32)
            rows[j, at : at + step, :] = (val * scale * gains[j][0:1, :]).astype(BF)
    hid = wide[0].shape[1]
    for j in range(4):
        start = pl.multiple_of(lax.rem(x + j, 4) * quarter, quarter)
        lhs = rows[j]
        for i in range(4):
            acc = gate_acc if i < 2 else up_acc
            cols = slice((i % 2) * hid, (i % 2 + 1) * hid)
            val = jnp.dot(lhs, wide[i][pl.ds(start, quarter), :], preferred_element_type=F32)
            if j == 0:
                acc[:, cols] = val
            else:
                acc[:, cols] += val
    gate = gate_acc[...]
    act[...] = (gate / (1.0 + jnp.exp(-gate)) * up_acc[...]).astype(BF)
    for j in range(4):
        start = pl.multiple_of(lax.rem(x + j, 4) * quarter, quarter)
        val = jnp.dot(act[:, :hid], down[0][:, pl.ds(start, quarter)], preferred_element_type=F32)
        val = val + jnp.dot(act[:, hid:], down[1][:, pl.ds(start, quarter)], preferred_element_type=F32)
        val = val.astype(BF)
        if j == 2:
            split = outs[2].shape[0]
            outs[2][...] = val[:split]
            outs[3][...] = val[split:]
        else:
            outs[j + j // 3][...] = val


def ffn(x, pieces, gains, wide, down):
    counts = tuple(tuple(p.shape[0] for p in per_j) for per_j in pieces)
    count = sum(counts[0])
    quarter = pieces[0][0].shape[1]
    hid = wide[0].shape[1]
    vmem = pl.BlockSpec(memory_space=pltpu.VMEM)
    n_pieces = sum(len(per_j) for per_j in counts)
    flops = 2 * count * 4 * quarter * 2 * hid * 3
    first = half_of(count)
    heights = [count, count, first, count - first, count]
    return pl.pallas_call(
        functools.partial(ffn_kernel, counts),
        out_shape=[jax.ShapeDtypeStruct((h, quarter), BF) for h in heights],
        in_specs=[pl.BlockSpec(memory_space=pltpu.SMEM)] + [vmem] * (n_pieces + 10),
        out_specs=[vmem] * 5,
        scratch_shapes=[
            pltpu.VMEM((4, count, quarter), BF),
            pltpu.VMEM((count, 2 * hid), BF),
            pltpu.VMEM((count, 2 * hid), F32),
            pltpu.VMEM((count, 2 * hid), F32),
        ],
        compiler_params=pltpu.CompilerParams(vmem_limit_bytes=13 * 1024 * 1024),
        cost_estimate=pl.CostEstimate(
            flops=flops, bytes_accessed=24 * quarter * hid * 2, transcendentals=count * 2 * hid
        ),
    )(x, *[p for per_j in pieces for p in per_j], *gains, *wide, *down)


def half_of(count):
    return (count // 32) * 16


def gather_x_first(a):
    return shift(a, "x", 1), shift(a, "x", -1)


def gather_x_last(a, left, right):
    h = half_of(a.shape[0])
    return [[a], [right], [shift(left[:h], "x", 1), shift(right[h:], "x", -1)], [left]]


def concat_rows(parts):
    def kernel(*refs):
        at = 0
        for ref in refs[:-1]:
            refs[-1][at : at + ref.shape[0], :] = ref[...]
            at += ref.shape[0]

    vmem = pl.BlockSpec(memory_space=pltpu.VMEM)
    shape = jax.ShapeDtypeStruct((sum(p.shape[0] for p in parts), parts[0].shape[1]), parts[0].dtype)
    params = pltpu.CompilerParams(vmem_limit_bytes=4 * 1024 * 1024)
    return pl.pallas_call(
        kernel, out_shape=shape, in_specs=[vmem] * len(parts), out_specs=vmem, compiler_params=params
    )(*parts)


def load_weights(weights):
    def kernel(*refs):
        n = len(refs) // 2
        copies = [pltpu.make_async_copy(refs[i], refs[n + i], refs[-1].at[i]) for i in range(n)]
        for copy in copies:
            copy.start()
        for copy in copies:
            copy.wait()

    n = len(weights)
    total = sum(w.size for w in weights) * 2
    return pl.pallas_call(
        kernel,
        out_shape=[jax.ShapeDtypeStruct(w.shape, w.dtype) for w in weights],
        in_specs=[pl.BlockSpec(memory_space=pl.ANY)] * n,
        out_specs=[pl.BlockSpec(memory_space=pltpu.VMEM)] * n,
        scratch_shapes=[pltpu.SemaphoreType.DMA((n,))],
        compiler_params=pltpu.CompilerParams(vmem_limit_bytes=4 * 1024 * 1024),
        cost_estimate=pl.CostEstimate(flops=0, bytes_accessed=2 * total, transcendentals=0),
    )(*weights)


def concat_far(p3, m3, p4, m4):
    def kernel(p3_ref, m3_ref, p4_ref, m4_ref, out_ref):
        n, half = p4_ref.shape
        out_ref[:n, :] = p3_ref[...]
        out_ref[n : 2 * n, :] = m3_ref[...]
        out_ref[2 * n :, :half] = p4_ref[...]
        out_ref[2 * n :, half:] = m4_ref[...]

    vmem = pl.BlockSpec(memory_space=pltpu.VMEM)
    shape = jax.ShapeDtypeStruct((3 * p3.shape[0], p3.shape[1]), p3.dtype)
    params = pltpu.CompilerParams(vmem_limit_bytes=4 * 1024 * 1024)
    return pl.pallas_call(
        kernel, out_shape=shape, in_specs=[vmem] * 4, out_specs=vmem, compiler_params=params
    )(p3, m3, p4, m4)


def add_rows(base, part, at):
    def kernel(base_ref, part_ref, out_ref):
        del base_ref
        rows = slice(at, at + part.shape[0])
        out_ref[rows, :] = (out_ref[rows, :].astype(F32) + part_ref[...].astype(F32)).astype(BF)

    vmem = pl.BlockSpec(memory_space=pltpu.VMEM)
    return pl.pallas_call(
        kernel,
        out_shape=jax.ShapeDtypeStruct(base.shape, base.dtype),
        in_specs=[vmem, vmem],
        out_specs=vmem,
        input_output_aliases={0: 0},
        compiler_params=pltpu.CompilerParams(vmem_limit_bytes=4 * 1024 * 1024),
    )(base, part)


def reduce_x_first(outs):
    _, to_right, far_first, far_second, to_left = outs
    h = far_first.shape[0]
    return add_rows(to_right, shift(far_first, "x", 1), 0), add_rows(to_left, shift(far_second, "x", -1), h)


def reduce_x_last(mine, right_sum, left_sum):
    from_left = shift(right_sum, "x", 1)
    from_right = shift(left_sum, "x", -1)
    return mine.astype(F32) + from_left.astype(F32) + from_right.astype(F32)


def body(tokens, gains, w_gate, w_up, w_down, expert_ids, gate_ints):
    z = lax.axis_index("z")
    x = lax.axis_index("x")
    c = lax.axis_index("c")
    y = lax.axis_index("y")
    tok, quarter = tokens.shape
    gate_w, up_w, down_w = w_gate[0], w_up[0], w_down[0]
    blocks = []
    for k in range(4):
        pairs = [(a * 4 + b, b * 4 + (a + k) % 4) for a in range(4) for b in range(4)]
        blocks.append(lax.ppermute(tokens, ("x", "y"), pairs))
    def routed_rows(a):
        starts = [((z * 4 + (y - k) % 4) * 2 + c) * tok for k in range(4)]
        return jnp.concatenate([lax.dynamic_slice_in_dim(a, start, tok, 0) for start in starts], axis=0)

    chosen = routed_rows(expert_ids) == y
    selected = jnp.any(chosen, axis=-1)
    weight = jnp.sum(jnp.where(chosen, routed_rows(gate_ints).astype(F32) / 65536.0, 0.0), axis=-1)
    col = jnp.arange(4 * tok)
    earlier = (col[None, :] // tok == col[:, None] // tok) & (col[None, :] < col[:, None])
    place = jnp.sum(earlier & selected[None, :], axis=1)
    slot = (y - col // tok) % 4 * CAP + place
    hot = (slot[None, :] == jnp.arange(4 * CAP)[:, None]) & selected[None, :]
    pick = hot.astype(BF)
    put = jnp.where(hot, weight[None, :], 0.0)

    picked = jnp.dot(pick, jnp.concatenate(blocks, axis=0), preferred_element_type=F32).astype(BF)
    gains_rel = [
        lax.broadcast_in_dim(lax.dynamic_slice_in_dim(gains, (x + j) % 4 * quarter, quarter, 0), (8, quarter), (1,))
        for j in range(4)
    ]
    x_arr = x.astype(jnp.int32).reshape(1)
    picked, put, x_arr, gains_rel, gate_s, up_in = lax.optimization_barrier(
        (picked, put, x_arr, gains_rel, shift(gate_w, "c", 1), up_w)
    )
    p1, m1 = shift(picked, "z", -1), shift(picked, "z", 1)
    p1, m1, up_s, down_in = lax.optimization_barrier((p1, m1, shift(up_in, "c", 1), down_w))
    gate_v, up_v, down_v = load_weights([gate_w, up_w, down_w])
    first = concat_rows([picked, p1, m1])
    first_left, first_right = gather_x_first(first)
    p2, m2 = shift(p1, "z", -1), shift(m1, "z", 1)
    p2, m2, down_s = lax.optimization_barrier((p2, m2, shift(down_in, "c", 1)))
    wide = [gate_v, gate_s, up_v, up_s]
    down = [down_v, down_s]
    second = concat_rows([p2, m2])
    second_left, second_right = gather_x_first(second)
    half = quarter // 2
    p3, m3 = shift(p2, "z", -1), shift(m2, "z", 1)
    p4, m4 = shift(p3[:, :half], "z", -1), shift(m3[:, half:], "z", 1)
    far = concat_far(p3, m3, p4, m4)
    far_left, far_right = gather_x_first(far)
    first = gather_x_last(first, first_left, first_right)
    second = gather_x_last(second, second_left, second_right)
    far = gather_x_last(far, far_left, far_right)

    near = [first[j] + second[j] for j in range(4)]
    out_near = ffn(x_arr, near, gains_rel, wide, down)
    sums_near = reduce_x_first(out_near)
    x_far, own_near = lax.optimization_barrier((x_arr, out_near[0]))
    out_far = ffn(x_far, far, gains_rel, wide, down)
    sums_near, out_far = lax.optimization_barrier((sums_near, out_far))

    n = picked.shape[0]
    sum_far = reduce_x_last(out_far[0], *reduce_x_first(out_far)).astype(BF)
    sum_near = reduce_x_last(own_near, *sums_near)
    slots = sum_near[:n]
    for i, by in enumerate((3, -3, 4)):
        slots = slots + shift(sum_far[i * n : (i + 1) * n], "z", by).astype(F32)
    for i, by in enumerate((1, -1, 2, -2)):
        slots = slots + shift(sum_near[(i + 1) * n : (i + 2) * n].astype(BF), "z", by).astype(F32)
    terms = lax.dot_general(
        put, slots, (((0,), (0,)), ((), ())), precision=lax.Precision.HIGHEST, preferred_element_type=F32
    ).astype(BF)
    total = tokens.astype(F32)
    for k in range(4):
        pairs = [(a * 4 + e, ((e - k) % 4) * 4 + a) for a in range(4) for e in range(4)]
        total = total + lax.ppermute(terms[k * tok : (k + 1) * tok], ("x", "y"), pairs).astype(F32)
    return total.astype(BF)


def solution(mesh):
    fine = Mesh(mesh.devices.reshape(8, 4, 2, 4), ("z", "x", "c", "y"))
    section = ("z", "x", "c")
    in_specs = (
        P(section, "y"),
        P(),
        P("y", None, section),
        P("y", None, section),
        P("y", section, None),
        P(),
        P(),
    )
    return jax.shard_map(body, mesh=fine, in_specs=in_specs, out_specs=P(section, "y"), check_vma=False)
```

```python
import functools

import jax
import jax.numpy as jnp
from jax import lax
from jax.experimental import pallas as pl
from jax.experimental.pallas import tpu as pltpu
from jax.sharding import Mesh, PartitionSpec as P

CAP = 12
BF = jnp.bfloat16
F32 = jnp.float32


def shift(a, axis, by):
    n = lax.axis_size(axis)
    return lax.ppermute(a, axis, [(i, (i + by) % n) for i in range(n)])


def ffn_kernel(counts, x_ref, *refs):
    refs = list(refs)
    pieces = [[refs.pop(0) for _ in per_j] for per_j in counts]
    gains, refs = refs[:4], refs[4:]
    wide, refs = refs[:4], refs[4:]
    down, refs = refs[:2], refs[2:]
    outs, refs = refs[:5], refs[5:]
    rows, act, gate_acc, up_acc = refs
    _, total_rows, quarter = rows.shape
    x = x_ref[0]
    for j in range(4):
        at = 0
        for piece, count in zip(pieces[j], counts[j]):
            rows[j, at : at + count, :] = piece[...]
            at += count
    step = 48
    for at in range(0, total_rows, step):
        total = jnp.zeros((step, 1), F32)
        for j in range(4):
            val = rows[j, at : at + step, :].astype(F32)
            total = total + jnp.sum(val * val, axis=1, keepdims=True)
        scale = lax.rsqrt(total / (4.0 * quarter) + 1e-05)
        for j in range(4):
            val = rows[j, at : at + step, :].astype(F32)
            rows[j, at : at + step, :] = (val * scale * gains[j][0:1, :]).astype(BF)
    hid = wide[0].shape[1]
    for j in range(4):
        start = pl.multiple_of(lax.rem(x + j, 4) * quarter, quarter)
        lhs = rows[j]
        for i in range(4):
            acc = gate_acc if i < 2 else up_acc
            cols = slice((i % 2) * hid, (i % 2 + 1) * hid)
            val = jnp.dot(lhs, wide[i][pl.ds(start, quarter), :], preferred_element_type=F32)
            if j == 0:
                acc[:, cols] = val
            else:
                acc[:, cols] += val
    gate = gate_acc[...]
    act[...] = (gate / (1.0 + jnp.exp(-gate)) * up_acc[...]).astype(BF)
    for j in range(4):
        start = pl.multiple_of(lax.rem(x + j, 4) * quarter, quarter)
        val = jnp.dot(act[:, :hid], down[0][:, pl.ds(start, quarter)], preferred_element_type=F32)
        val = val + jnp.dot(act[:, hid:], down[1][:, pl.ds(start, quarter)], preferred_element_type=F32)
        val = val.astype(BF)
        if j == 2:
            split = outs[2].shape[0]
            outs[2][...] = val[:split]
            outs[3][...] = val[split:]
        else:
            outs[j + j // 3][...] = val


def ffn(x, pieces, gains, wide, down):
    counts = tuple(tuple(p.shape[0] for p in per_j) for per_j in pieces)
    count = sum(counts[0])
    quarter = pieces[0][0].shape[1]
    hid = wide[0].shape[1]
    vmem = pl.BlockSpec(memory_space=pltpu.VMEM)
    n_pieces = sum(len(per_j) for per_j in counts)
    flops = 2 * count * 4 * quarter * 2 * hid * 3
    first = half_of(count)
    heights = [count, count, first, count - first, count]
    return pl.pallas_call(
        functools.partial(ffn_kernel, counts),
        out_shape=[jax.ShapeDtypeStruct((h, quarter), BF) for h in heights],
        in_specs=[pl.BlockSpec(memory_space=pltpu.SMEM)] + [vmem] * (n_pieces + 10),
        out_specs=[vmem] * 5,
        scratch_shapes=[
            pltpu.VMEM((4, count, quarter), BF),
            pltpu.VMEM((count, 2 * hid), BF),
            pltpu.VMEM((count, 2 * hid), F32),
            pltpu.VMEM((count, 2 * hid), F32),
        ],
        compiler_params=pltpu.CompilerParams(vmem_limit_bytes=13 * 1024 * 1024),
        cost_estimate=pl.CostEstimate(
            flops=flops, bytes_accessed=24 * quarter * hid * 2, transcendentals=count * 2 * hid
        ),
    )(x, *[p for per_j in pieces for p in per_j], *gains, *wide, *down)


def half_of(count):
    return (count // 32) * 16


def gather_x_first(a):
    return shift(a, "x", 1), shift(a, "x", -1)


def gather_x_last(a, left, right):
    h = half_of(a.shape[0])
    return [[a], [right], [shift(left[:h], "x", 1), shift(right[h:], "x", -1)], [left]]


def concat_rows(parts):
    def kernel(*refs):
        at = 0
        for ref in refs[:-1]:
            refs[-1][at : at + ref.shape[0], :] = ref[...]
            at += ref.shape[0]

    vmem = pl.BlockSpec(memory_space=pltpu.VMEM)
    shape = jax.ShapeDtypeStruct((sum(p.shape[0] for p in parts), parts[0].shape[1]), parts[0].dtype)
    params = pltpu.CompilerParams(vmem_limit_bytes=4 * 1024 * 1024)
    return pl.pallas_call(
        kernel, out_shape=shape, in_specs=[vmem] * len(parts), out_specs=vmem, compiler_params=params
    )(*parts)


def load_weights(weights):
    def kernel(*refs):
        n = len(refs) // 2
        copies = [pltpu.make_async_copy(refs[i], refs[n + i], refs[-1].at[i]) for i in range(n)]
        for copy in copies:
            copy.start()
        for copy in copies:
            copy.wait()

    n = len(weights)
    total = sum(w.size for w in weights) * 2
    return pl.pallas_call(
        kernel,
        out_shape=[jax.ShapeDtypeStruct(w.shape, w.dtype) for w in weights],
        in_specs=[pl.BlockSpec(memory_space=pl.ANY)] * n,
        out_specs=[pl.BlockSpec(memory_space=pltpu.VMEM)] * n,
        scratch_shapes=[pltpu.SemaphoreType.DMA((n,))],
        compiler_params=pltpu.CompilerParams(vmem_limit_bytes=45 * 1024 * 1024),
        cost_estimate=pl.CostEstimate(flops=0, bytes_accessed=2 * total, transcendentals=0),
    )(*weights)


def concat_far(p3, m3, p4, m4):
    def kernel(p3_ref, m3_ref, p4_ref, m4_ref, out_ref):
        n, half = p4_ref.shape
        out_ref[:n, :] = p3_ref[...]
        out_ref[n : 2 * n, :] = m3_ref[...]
        out_ref[2 * n :, :half] = p4_ref[...]
        out_ref[2 * n :, half:] = m4_ref[...]

    vmem = pl.BlockSpec(memory_space=pltpu.VMEM)
    shape = jax.ShapeDtypeStruct((3 * p3.shape[0], p3.shape[1]), p3.dtype)
    params = pltpu.CompilerParams(vmem_limit_bytes=4 * 1024 * 1024)
    return pl.pallas_call(
        kernel, out_shape=shape, in_specs=[vmem] * 4, out_specs=vmem, compiler_params=params
    )(p3, m3, p4, m4)


def add_rows(base, part, at):
    def kernel(base_ref, part_ref, out_ref):
        del base_ref
        rows = slice(at, at + part.shape[0])
        out_ref[rows, :] = (out_ref[rows, :].astype(F32) + part_ref[...].astype(F32)).astype(BF)

    vmem = pl.BlockSpec(memory_space=pltpu.VMEM)
    return pl.pallas_call(
        kernel,
        out_shape=jax.ShapeDtypeStruct(base.shape, base.dtype),
        in_specs=[vmem, vmem],
        out_specs=vmem,
        input_output_aliases={0: 0},
        compiler_params=pltpu.CompilerParams(vmem_limit_bytes=4 * 1024 * 1024),
    )(base, part)


def reduce_x_first(outs):
    _, to_right, far_first, far_second, to_left = outs
    h = far_first.shape[0]
    return add_rows(to_right, shift(far_first, "x", 1), 0), add_rows(to_left, shift(far_second, "x", -1), h)


def reduce_x_last(mine, right_sum, left_sum):
    from_left = shift(right_sum, "x", 1)
    from_right = shift(left_sum, "x", -1)
    return mine.astype(F32) + from_left.astype(F32) + from_right.astype(F32)


def body(tokens, gains, w_gate, w_up, w_down, expert_ids, gate_ints):
    z = lax.axis_index("z")
    x = lax.axis_index("x")
    c = lax.axis_index("c")
    y = lax.axis_index("y")
    tok, quarter = tokens.shape
    gate_w, up_w, down_w = w_gate[0], w_up[0], w_down[0]
    blocks = []
    for k in range(4):
        pairs = [(a * 4 + b, b * 4 + (a + k) % 4) for a in range(4) for b in range(4)]
        blocks.append(lax.ppermute(tokens, ("x", "y"), pairs))
    def routed_rows(a):
        starts = [((z * 4 + (y - k) % 4) * 2 + c) * tok for k in range(4)]
        return jnp.concatenate([lax.dynamic_slice_in_dim(a, start, tok, 0) for start in starts], axis=0)

    chosen = routed_rows(expert_ids) == y
    selected = jnp.any(chosen, axis=-1)
    weight = jnp.sum(jnp.where(chosen, routed_rows(gate_ints).astype(F32) / 65536.0, 0.0), axis=-1)
    col = jnp.arange(4 * tok)
    earlier = (col[None, :] // tok == col[:, None] // tok) & (col[None, :] < col[:, None])
    place = jnp.sum(earlier & selected[None, :], axis=1)
    slot = (y - col // tok) % 4 * CAP + place
    hot = (slot[None, :] == jnp.arange(4 * CAP)[:, None]) & selected[None, :]
    pick = hot.astype(BF)
    put = jnp.where(hot, weight[None, :], 0.0)

    picked = jnp.dot(pick, jnp.concatenate(blocks, axis=0), preferred_element_type=F32).astype(BF)
    gains_rel = [
        lax.broadcast_in_dim(lax.dynamic_slice_in_dim(gains, (x + j) % 4 * quarter, quarter, 0), (8, quarter), (1,))
        for j in range(4)
    ]
    x_arr = x.astype(jnp.int32).reshape(1)
    picked, put, x_arr, gains_rel, gate_s, up_in = lax.optimization_barrier(
        (picked, put, x_arr, gains_rel, shift(gate_w, "c", 1), up_w)
    )
    p1, m1 = shift(picked, "z", -1), shift(picked, "z", 1)
    gate_v, up_v, down_v = load_weights([gate_w, up_w, down_w])
    p1, m1, up_s, down_in, gate_v, up_v, down_v = lax.optimization_barrier(
        (p1, m1, shift(up_in, "c", 1), down_w, gate_v, up_v, down_v)
    )
    first = concat_rows([picked, p1, m1])
    first_left, first_right = gather_x_first(first)
    p2, m2 = shift(p1, "z", -1), shift(m1, "z", 1)
    p2, m2, down_s = lax.optimization_barrier((p2, m2, shift(down_in, "c", 1)))
    wide = [gate_v, gate_s, up_v, up_s]
    down = [down_v, down_s]
    second = concat_rows([p2, m2])
    second_left, second_right = gather_x_first(second)
    half = quarter // 2
    p3, m3 = shift(p2, "z", -1), shift(m2, "z", 1)
    p4, m4 = shift(p3[:, :half], "z", -1), shift(m3[:, half:], "z", 1)
    p4, m4, second_left, second_right = lax.optimization_barrier((p4, m4, second_left, second_right))
    far = concat_far(p3, m3, p4, m4)
    far_left, far_right = gather_x_first(far)
    first = gather_x_last(first, first_left, first_right)
    second = gather_x_last(second, second_left, second_right)
    far = gather_x_last(far, far_left, far_right)

    near = [first[j] + second[j] for j in range(4)]
    out_near = ffn(x_arr, near, gains_rel, wide, down)
    sums_near = reduce_x_first(out_near)
    x_far, own_near = lax.optimization_barrier((x_arr, out_near[0]))
    out_far = ffn(x_far, far, gains_rel, wide, down)
    sums_near, out_far = lax.optimization_barrier((sums_near, out_far))

    n = picked.shape[0]
    sum_far = reduce_x_last(out_far[0], *reduce_x_first(out_far)).astype(BF)
    sum_near = reduce_x_last(own_near, *sums_near)
    slots = sum_near[:n]
    for i, by in enumerate((3, -3, 4)):
        slots = slots + shift(sum_far[i * n : (i + 1) * n], "z", by).astype(F32)
    for i, by in enumerate((1, -1, 2, -2)):
        slots = slots + shift(sum_near[(i + 1) * n : (i + 2) * n].astype(BF), "z", by).astype(F32)
    terms = lax.dot_general(
        put, slots, (((0,), (0,)), ((), ())), precision=lax.Precision.HIGHEST, preferred_element_type=F32
    ).astype(BF)
    total = tokens.astype(F32)
    for k in range(4):
        pairs = [(a * 4 + e, ((e - k) % 4) * 4 + a) for a in range(4) for e in range(4)]
        total = total + lax.ppermute(terms[k * tok : (k + 1) * tok], ("x", "y"), pairs).astype(F32)
    return total.astype(BF)


def solution(mesh):
    fine = Mesh(mesh.devices.reshape(8, 4, 2, 4), ("z", "x", "c", "y"))
    section = ("z", "x", "c")
    in_specs = (
        P(section, "y"),
        P(),
        P("y", None, section),
        P("y", None, section),
        P("y", section, None),
        P(),
        P(),
    )
    return jax.shard_map(body, mesh=fine, in_specs=in_specs, out_specs=P(section, "y"), check_vma=False)
```

```python
import functools

import jax
import jax.numpy as jnp
from jax import lax
from jax.experimental import pallas as pl
from jax.experimental.pallas import tpu as pltpu
from jax.sharding import Mesh, PartitionSpec as P

CAP = 12
BF = jnp.bfloat16
F32 = jnp.float32


def shift(a, axis, by):
    n = lax.axis_size(axis)
    return lax.ppermute(a, axis, [(i, (i + by) % n) for i in range(n)])


def ffn_kernel(counts, x_ref, *refs):
    refs = list(refs)
    pieces = [[refs.pop(0) for _ in per_j] for per_j in counts]
    gains, refs = refs[:4], refs[4:]
    wide, refs = refs[:4], refs[4:]
    down, refs = refs[:2], refs[2:]
    outs, refs = refs[:5], refs[5:]
    rows, act, gate_acc, up_acc = refs
    _, total_rows, quarter = rows.shape
    x = x_ref[0]
    for j in range(4):
        at = 0
        for piece, count in zip(pieces[j], counts[j]):
            rows[j, at : at + count, :] = piece[...]
            at += count
    step = 48
    for at in range(0, total_rows, step):
        total = jnp.zeros((step, 1), F32)
        for j in range(4):
            val = rows[j, at : at + step, :].astype(F32)
            total = total + jnp.sum(val * val, axis=1, keepdims=True)
        scale = lax.rsqrt(total / (4.0 * quarter) + 1e-05)
        for j in range(4):
            val = rows[j, at : at + step, :].astype(F32)
            rows[j, at : at + step, :] = (val * scale * gains[j][0:1, :]).astype(BF)
    hid = wide[0].shape[1]
    for j in range(4):
        start = pl.multiple_of(lax.rem(x + j, 4) * quarter, quarter)
        lhs = rows[j]
        for i in range(4):
            acc = gate_acc if i < 2 else up_acc
            cols = slice((i % 2) * hid, (i % 2 + 1) * hid)
            val = jnp.dot(lhs, wide[i][pl.ds(start, quarter), :], preferred_element_type=F32)
            if j == 0:
                acc[:, cols] = val
            else:
                acc[:, cols] += val
    gate = gate_acc[...]
    act[...] = (gate / (1.0 + jnp.exp(-gate)) * up_acc[...]).astype(BF)
    for j in range(4):
        start = pl.multiple_of(lax.rem(x + j, 4) * quarter, quarter)
        val = jnp.dot(act[:, :hid], down[0][:, pl.ds(start, quarter)], preferred_element_type=F32)
        val = val + jnp.dot(act[:, hid:], down[1][:, pl.ds(start, quarter)], preferred_element_type=F32)
        val = val.astype(BF)
        if j == 2:
            split = outs[2].shape[0]
            outs[2][...] = val[:split]
            outs[3][...] = val[split:]
        else:
            outs[j + j // 3][...] = val


def ffn(x, pieces, gains, wide, down):
    counts = tuple(tuple(p.shape[0] for p in per_j) for per_j in pieces)
    count = sum(counts[0])
    quarter = pieces[0][0].shape[1]
    hid = wide[0].shape[1]
    vmem = pl.BlockSpec(memory_space=pltpu.VMEM)
    n_pieces = sum(len(per_j) for per_j in counts)
    flops = 2 * count * 4 * quarter * 2 * hid * 3
    first = half_of(count)
    heights = [count, count, first, count - first, count]
    return pl.pallas_call(
        functools.partial(ffn_kernel, counts),
        out_shape=[jax.ShapeDtypeStruct((h, quarter), BF) for h in heights],
        in_specs=[pl.BlockSpec(memory_space=pltpu.SMEM)] + [vmem] * (n_pieces + 10),
        out_specs=[vmem] * 5,
        scratch_shapes=[
            pltpu.VMEM((4, count, quarter), BF),
            pltpu.VMEM((count, 2 * hid), BF),
            pltpu.VMEM((count, 2 * hid), F32),
            pltpu.VMEM((count, 2 * hid), F32),
        ],
        compiler_params=pltpu.CompilerParams(vmem_limit_bytes=13 * 1024 * 1024),
        cost_estimate=pl.CostEstimate(
            flops=flops, bytes_accessed=24 * quarter * hid * 2, transcendentals=count * 2 * hid
        ),
    )(x, *[p for per_j in pieces for p in per_j], *gains, *wide, *down)


def half_of(count):
    return (count // 32) * 16


def gather_x_first(a):
    return shift(a, "x", 1), shift(a, "x", -1)


def gather_x_last(a, left, right):
    h = half_of(a.shape[0])
    return [[a], [right], [shift(left[:h], "x", 1), shift(right[h:], "x", -1)], [left]]


def concat_rows(parts):
    def kernel(*refs):
        at = 0
        for ref in refs[:-1]:
            refs[-1][at : at + ref.shape[0], :] = ref[...]
            at += ref.shape[0]

    vmem = pl.BlockSpec(memory_space=pltpu.VMEM)
    shape = jax.ShapeDtypeStruct((sum(p.shape[0] for p in parts), parts[0].shape[1]), parts[0].dtype)
    params = pltpu.CompilerParams(vmem_limit_bytes=4 * 1024 * 1024)
    return pl.pallas_call(
        kernel, out_shape=shape, in_specs=[vmem] * len(parts), out_specs=vmem, compiler_params=params
    )(*parts)


def load_weights(weights):
    def kernel(*refs):
        n = len(refs) // 2
        copies = [pltpu.make_async_copy(refs[i], refs[n + i], refs[-1].at[i]) for i in range(n)]
        for copy in copies:
            copy.start()
        for copy in copies:
            copy.wait()

    n = len(weights)
    total = sum(w.size for w in weights) * 2
    return pl.pallas_call(
        kernel,
        out_shape=[jax.ShapeDtypeStruct(w.shape, w.dtype) for w in weights],
        in_specs=[pl.BlockSpec(memory_space=pl.ANY)] * n,
        out_specs=[pl.BlockSpec(memory_space=pltpu.VMEM)] * n,
        scratch_shapes=[pltpu.SemaphoreType.DMA((n,))],
        compiler_params=pltpu.CompilerParams(vmem_limit_bytes=45 * 1024 * 1024),
        cost_estimate=pl.CostEstimate(flops=0, bytes_accessed=2 * total, transcendentals=0),
    )(*weights)


def concat_far(p3, m3, p4, m4):
    def kernel(p3_ref, m3_ref, p4_ref, m4_ref, out_ref):
        n, half = p4_ref.shape
        out_ref[:n, :] = p3_ref[...]
        out_ref[n : 2 * n, :] = m3_ref[...]
        out_ref[2 * n :, :half] = p4_ref[...]
        out_ref[2 * n :, half:] = m4_ref[...]

    vmem = pl.BlockSpec(memory_space=pltpu.VMEM)
    shape = jax.ShapeDtypeStruct((3 * p3.shape[0], p3.shape[1]), p3.dtype)
    params = pltpu.CompilerParams(vmem_limit_bytes=4 * 1024 * 1024)
    return pl.pallas_call(
        kernel, out_shape=shape, in_specs=[vmem] * 4, out_specs=vmem, compiler_params=params
    )(p3, m3, p4, m4)


def add_rows(base, part, at):
    def kernel(base_ref, part_ref, out_ref):
        del base_ref
        rows = slice(at, at + part.shape[0])
        out_ref[rows, :] = (out_ref[rows, :].astype(F32) + part_ref[...].astype(F32)).astype(BF)

    vmem = pl.BlockSpec(memory_space=pltpu.VMEM)
    return pl.pallas_call(
        kernel,
        out_shape=jax.ShapeDtypeStruct(base.shape, base.dtype),
        in_specs=[vmem, vmem],
        out_specs=vmem,
        input_output_aliases={0: 0},
        compiler_params=pltpu.CompilerParams(vmem_limit_bytes=4 * 1024 * 1024),
    )(base, part)


def reduce_x_first(outs):
    _, to_right, far_first, far_second, to_left = outs
    h = far_first.shape[0]
    return add_rows(to_right, shift(far_first, "x", 1), 0), add_rows(to_left, shift(far_second, "x", -1), h)


def reduce_x_last(mine, right_sum, left_sum):
    from_left = shift(right_sum, "x", 1)
    from_right = shift(left_sum, "x", -1)
    return mine.astype(F32) + from_left.astype(F32) + from_right.astype(F32)


def body(tokens, gains, w_gate, w_up, w_down, expert_ids, gate_ints):
    z = lax.axis_index("z")
    x = lax.axis_index("x")
    c = lax.axis_index("c")
    y = lax.axis_index("y")
    tok, quarter = tokens.shape
    gate_w, up_w, down_w = w_gate[0], w_up[0], w_down[0]
    blocks = []
    for k in range(4):
        pairs = [(a * 4 + b, b * 4 + (a + k) % 4) for a in range(4) for b in range(4)]
        blocks.append(lax.ppermute(tokens, ("x", "y"), pairs))
    def routed_rows(a):
        starts = [((z * 4 + (y - k) % 4) * 2 + c) * tok for k in range(4)]
        return jnp.concatenate([lax.dynamic_slice_in_dim(a, start, tok, 0) for start in starts], axis=0)

    chosen = routed_rows(expert_ids) == y
    selected = jnp.any(chosen, axis=-1)
    weight = jnp.sum(jnp.where(chosen, routed_rows(gate_ints).astype(F32) / 65536.0, 0.0), axis=-1)
    col = jnp.arange(4 * tok)
    earlier = (col[None, :] // tok == col[:, None] // tok) & (col[None, :] < col[:, None])
    place = jnp.sum(earlier & selected[None, :], axis=1)
    slot = (y - col // tok) % 4 * CAP + place
    hot = (slot[None, :] == jnp.arange(4 * CAP)[:, None]) & selected[None, :]
    pick = hot.astype(BF)
    put = jnp.where(hot, weight[None, :], 0.0)

    picked = jnp.dot(pick, jnp.concatenate(blocks, axis=0), preferred_element_type=F32).astype(BF)
    gains_rel = [
        lax.broadcast_in_dim(lax.dynamic_slice_in_dim(gains, (x + j) % 4 * quarter, quarter, 0), (8, quarter), (1,))
        for j in range(4)
    ]
    x_arr = x.astype(jnp.int32).reshape(1)
    picked, put, x_arr, gains_rel, gate_s, up_in = lax.optimization_barrier(
        (picked, put, x_arr, gains_rel, shift(gate_w, "c", 1), up_w)
    )
    p1, m1 = shift(picked, "z", -1), shift(picked, "z", 1)
    gate_v, up_v = load_weights([gate_w, up_w])
    p1, m1, up_s, down_in, gate_v, up_v = lax.optimization_barrier(
        (p1, m1, shift(up_in, "c", 1), down_w, gate_v, up_v)
    )
    first = concat_rows([picked, p1, m1])
    first_left, first_right = gather_x_first(first)
    p2, m2 = shift(p1, "z", -1), shift(m1, "z", 1)
    (down_v,) = load_weights([down_w])
    p2, m2, down_s, down_v = lax.optimization_barrier((p2, m2, shift(down_in, "c", 1), down_v))
    wide = [gate_v, gate_s, up_v, up_s]
    down = [down_v, down_s]
    second = concat_rows([p2, m2])
    second_left, second_right = gather_x_first(second)
    half = quarter // 2
    p3, m3 = shift(p2, "z", -1), shift(m2, "z", 1)
    p4, m4 = shift(p3[:, :half], "z", -1), shift(m3[:, half:], "z", 1)
    p4, m4, second_left, second_right = lax.optimization_barrier((p4, m4, second_left, second_right))
    far = concat_far(p3, m3, p4, m4)
    far_left, far_right = gather_x_first(far)
    first = gather_x_last(first, first_left, first_right)
    second = gather_x_last(second, second_left, second_right)
    far = gather_x_last(far, far_left, far_right)

    near = [first[j] + second[j] for j in range(4)]
    out_near = ffn(x_arr, near, gains_rel, wide, down)
    sums_near = reduce_x_first(out_near)
    x_far, own_near = lax.optimization_barrier((x_arr, out_near[0]))
    out_far = ffn(x_far, far, gains_rel, wide, down)
    sums_near, out_far = lax.optimization_barrier((sums_near, out_far))

    n = picked.shape[0]
    sum_far = reduce_x_last(out_far[0], *reduce_x_first(out_far)).astype(BF)
    sum_near = reduce_x_last(own_near, *sums_near)
    slots = sum_near[:n]
    for i, by in enumerate((3, -3, 4)):
        slots = slots + shift(sum_far[i * n : (i + 1) * n], "z", by).astype(F32)
    for i, by in enumerate((1, -1, 2, -2)):
        slots = slots + shift(sum_near[(i + 1) * n : (i + 2) * n].astype(BF), "z", by).astype(F32)
    terms = lax.dot_general(
        put, slots, (((0,), (0,)), ((), ())), precision=lax.Precision.HIGHEST, preferred_element_type=F32
    ).astype(BF)
    total = tokens.astype(F32)
    for k in range(4):
        pairs = [(a * 4 + e, ((e - k) % 4) * 4 + a) for a in range(4) for e in range(4)]
        total = total + lax.ppermute(terms[k * tok : (k + 1) * tok], ("x", "y"), pairs).astype(F32)
    return total.astype(BF)


def solution(mesh):
    fine = Mesh(mesh.devices.reshape(8, 4, 2, 4), ("z", "x", "c", "y"))
    section = ("z", "x", "c")
    in_specs = (
        P(section, "y"),
        P(),
        P("y", None, section),
        P("y", None, section),
        P("y", section, None),
        P(),
        P(),
    )
    return jax.shard_map(body, mesh=fine, in_specs=in_specs, out_specs=P(section, "y"), check_vma=False)
```
